32 devices in a mesh: tm: 16 (over z, y, x), space: 2 (over core).
Axes of the slice: x: 2, y: 2, z: 4, core: 2. Of those that a mesh axis runs over, the one named last changes fastest.
Arguments:
- traj: float32 [16, 32, 32, 128], P('tm', None, 'space'), may hold values from -6 to 6
- start_state: float32 [32, 32, 128], P(None, 'space'), may hold values from -6 to 6
- actions: float32 [16, 16], P('tm'), may hold values from -6 to 6
- hidden_w: bfloat16 [3, 9, 32, 32], replicated, may hold values from -0.375 to 0.375
- hidden_b: float32 [3, 32], replicated, may hold values from -3 to 3
- head_w: bfloat16 [9, 64, 32], replicated, may hold values from -0.375 to 0.375
- cand_b: float32 [32], replicated, may hold values from -3 to 3
- gate_b: float32 [32], replicated, may hold values from 0 to 9
- skip: float32 [32], replicated, may hold values from 0.1 to 0.9
- act_proj: float32 [16, 64], replicated, may hold values from -1.5 to 1.5
Outputs:
- new_traj: float32 [16, 32, 32, 128], P('tm', None, 'space')
- res_msq: float32 [16], P('tm')
The draws below stay inside these ranges and needn't reach their ends.
All inputs are finite; a program needn't handle non-finite values.
Results may differ from the reference program's by a relative error of at most 0.0015.
Values may be sent and summed in bfloat16 or wider, within the bound.
A program may use at most 128 MiB of HBM per device.

```python
import jax
import jax.numpy as jnp
from jax import lax

C = 32
W = 128
ACT = 16
HID_LAYERS = 3
STEPS_DEV = 1
HORIZON = 16
ROWS = 32
N_TM = 16


def level_of(rng, dims, cuts, least, top_value):
    def one(axis_at, blocks):
        draws = jax.random.uniform(jax.random.fold_in(jax.random.fold_in(rng, 6), axis_at), (blocks,), jnp.float32, least / len(cuts), top_value / len(cuts))
        return jnp.repeat(jnp.exp(draws), dims[axis_at] // blocks).reshape((-1,) + (1,) * (len(dims) - axis_at - 1))

    factor_of = one(*cuts[0])
    for cut in cuts[1:]:
        factor_of = factor_of * one(*cut)
    return factor_of


def normal_values(key, dims, deviation, limit, split=(), kind=jnp.bfloat16):
    entries = jax.random.normal(key, dims, jnp.float32) * deviation
    if len(split) > 0:
        entries = level_of(key, dims, split, -0.22, 0.18) * entries
    return jnp.clip(entries, min=-limit, max=limit).astype(kind)


def setup_inputs(seed: int = 0) -> dict:
    keys = jax.random.split(jax.random.key(seed), 11)
    return {
        "traj": normal_values(keys[0], (HORIZON, C, ROWS, W), 1.0, 6.0, ((0, 16), (2, 2)), jnp.float32),
        "start_state": normal_values(keys[1], (C, ROWS, W), 1.0, 6.0, ((1, 2),), jnp.float32),
        "actions": normal_values(keys[2], (HORIZON, ACT), 1.0, 6.0, ((0, 16),), jnp.float32),
        "hidden_w": normal_values(keys[3], (HID_LAYERS, 9, C, C), (9 * C) ** -0.5, 0.375),
        "hidden_b": normal_values(keys[4], (HID_LAYERS, C), 0.5, 3.0, (), jnp.float32),
        "head_w": normal_values(keys[5], (9, 2 * C, C), (9 * C) ** -0.5, 0.375),
        "cand_b": normal_values(keys[6], (C,), 0.5, 3.0, (), jnp.float32),
        "gate_b": jnp.clip(jax.random.uniform(keys[7], (C,), jnp.float32, 0.0, 9.0), 0.0, 9.0),
        "skip": jnp.clip(jax.random.uniform(keys[8], (C,), jnp.float32, 0.1, 0.9), 0.1, 0.9),
        "act_proj": normal_values(keys[9], (ACT, 2 * C), ACT ** -0.5, 1.5, (), jnp.float32),
    }


def conv_same(hidden, taps):
    outs = taps.shape[1]
    ins = taps.shape[2]
    kernel = taps.reshape(3, 3, outs, ins).transpose(2, 3, 0, 1)
    return lax.conv_general_dilated(hidden, kernel, (1, 1), ((1, 1), (1, 1)),
                                    dimension_numbers=("NCHW", "OIHW", "NCHW"),
                                    preferred_element_type=jnp.float32)


def dynamics(guess_in, acts, hidden_w, hidden_b, head_w, cand_b, gate_b, skip, act_proj):
    chans = guess_in.shape[1]
    act_terms = jnp.dot(acts, act_proj, precision=lax.Precision.HIGHEST, preferred_element_type=jnp.float32)
    hidden = guess_in.astype(jnp.bfloat16)
    for layer in range(HID_LAYERS):
        pre = conv_same(hidden, hidden_w[layer]) + hidden_b[layer][None, :, None, None]
        if layer == 0:
            pre = pre + act_terms[:, :chans, None, None]
        hidden = jax.nn.silu(pre).astype(jnp.bfloat16)
    head = conv_same(hidden, head_w)
    cand = jnp.tanh(head[:, :chans] + cand_b[None, :, None, None] + skip[None, :, None, None] * guess_in)
    gate = jax.nn.sigmoid(head[:, chans:] + gate_b[None, :, None, None] + act_terms[:, chans:, None, None])
    fval = gate * guess_in + (1.0 - gate) * cand
    jac = gate + (1.0 - gate) * (1.0 - cand * cand) * skip[None, :, None, None]
    return fval, jac


def reference(traj, start_state, actions, hidden_w, hidden_b, head_w, cand_b, gate_b, skip, act_proj):
    steps = STEPS_DEV
    blocks = traj.reshape(N_TM, steps, traj.shape[1], traj.shape[2], traj.shape[3])
    act_blocks = actions.reshape(N_TM, steps, actions.shape[1])

    def block_step(carry, item):
        last, state = carry
        blk, acts = item
        guess_in = jnp.concatenate([last[None], blk[:steps - 1]], axis=0)
        fval, jac = dynamics(guess_in, acts, hidden_w, hidden_b, head_w, cand_b, gate_b, skip, act_proj)
        resid = jnp.mean((blk - fval) ** 2, axis=(1, 2, 3))
        offs = fval - jac * guess_in

        def advance(yval, pair):
            nxt = pair[0] * yval + pair[1]
            return nxt, nxt

        state, ys = lax.scan(advance, state, (jac, offs))
        return (blk[steps - 1], state), (ys, resid)

    _, (ys, resid) = lax.scan(block_step, (start_state, start_state), (blocks, act_blocks))
    return ys.reshape(traj.shape), resid.reshape(actions.shape[0])
```

```python
import functools

import jax
import jax.numpy as jnp
from jax import lax
from jax.experimental import pallas as pl
from jax.experimental.pallas import tpu as pltpu
from jax.sharding import PartitionSpec as P

MESH = pl.DeviceIdType.MESH
Q = 2
PARTS = 4
VMEM = pltpu.VMEM


def column(row):
    n = row.shape[1]
    eye = lax.broadcasted_iota(jnp.int32, (n, n), 0) == lax.broadcasted_iota(jnp.int32, (n, n), 1)
    return jnp.sum(jnp.where(eye, jnp.broadcast_to(row, (n, n)), 0.0), axis=1, keepdims=True)


def kernel(
    T, S, G, K, C, R, W, layers,
    traj_h, start_h, actions, hw, hb, headw, cand_b, gate_b, skip_r, proj,
    out, res,
    traj, start, sendb, ext, ha, hbuf, wh, wo, start_r, guess, ab, rab, cin, cout, ys, st, part, rpart,
    s_in, s_prior, r_prior, s_ab, r_ab, s_ch, r_ch, s_st, r_st, s_ps, r_ps,
):
    H = layers + 1
    L = R * C // G
    CH = L // K
    NG = T // G
    RG = R // G
    t = lax.axis_index("tm")
    s = lax.axis_index("space")
    g = t // G
    m = lax.rem(t, G)
    base = g * G
    nxt, prv = lax.rem(t + 1, T), lax.rem(t + T - 1, T)
    peers = []
    for tt in (nxt, prv):
        for ds in sorted({0, 1 % S, (S - 1) % S}):
            peers.append((tt, lax.rem(s + ds, S)))
    for p in range(1, G):
        peers.append((base + lax.rem(m + p, G), s))
    for step in (G, T - G):
        if NG > 1:
            peers.append((lax.rem(t + step, T), s))
    for p in range(1, S):
        peers.append((t, lax.rem(s + p, S)))
    load_t = pltpu.make_async_copy(traj_h, traj, s_in.at[0])
    load_s = pltpu.make_async_copy(start_h, start, s_in.at[1])
    load_t.start()
    load_s.start()
    barrier = pltpu.get_barrier_semaphore()
    for peer in peers:
        pl.semaphore_signal(barrier, inc=1, device_id=peer, device_id_type=MESH)

    last = t == T - 1
    load_t.wait()
    load_s.wait()
    for r in range(R):
        begin = start[pl.ds(r, C, stride=R), :]
        start_r[pl.ds(r * C, C), :] = begin
        sendb[pl.ds(r * C, C), :] = jnp.where(last, begin, traj[pl.ds(r, C, stride=R), :]).astype(jnp.bfloat16)

    pl.semaphore_wait(barrier, len(peers))

    def prior_copy(i, src, dst, to):
        return pltpu.make_async_remote_copy(
            src_ref=src, dst_ref=dst, send_sem=s_prior.at[i], recv_sem=r_prior.at[i],
            device_id=(nxt, to), device_id_type=MESH)

    up, down = s > 0, s < S - 1
    to_down = prior_copy(0, sendb.at[pl.ds((R - H) * C, H * C)], ext.at[pl.ds(0, H * C)], lax.rem(s + 1, S))
    to_up = prior_copy(1, sendb.at[pl.ds(0, H * C)], ext.at[pl.ds((R + H) * C, H * C)], lax.rem(s + S - 1, S))
    PR = R // PARTS
    main = [
        prior_copy(2 + i, sendb.at[pl.ds(i * PR * C, PR * C)], ext.at[pl.ds((H + i * PR) * C, PR * C)], s)
        for i in range(PARTS)
    ]

    @pl.when(down)
    def _():
        to_down.start()

    for copy in main:
        copy.start()

    @pl.when(up)
    def _():
        to_up.start()

    wh[...] = jnp.zeros_like(wh)
    wo[...] = jnp.zeros_like(wo)
    taps = [headw[pl.ds(k * C, C), :].astype(jnp.float32).T.astype(jnp.bfloat16) for k in range(9)]
    for q in range(Q):
        for a in range(3):
            for b in range(3):
                at = ((q + a) * 3 + b) * C
                for l in range(layers):
                    wh[l, pl.ds(q * C, C), pl.ds(at, C)] = hw[pl.ds((l * 9 + 3 * a + b) * C, C), :]
                wo[pl.ds(q * 2 * C, 2 * C), pl.ds(at, C)] = taps[3 * a + b]
    act = column(jnp.sum(column(actions[...]) * proj[...], axis=0, keepdims=True))
    biases = [column(hb[pl.ds(l, 1), :]) for l in range(layers)]
    biases[0] = biases[0] + act[:C]
    cb = column(cand_b[...])
    gb = column(gate_b[...]) + act[C:]
    skip = column(skip_r[...])
    lane = lax.broadcasted_iota(jnp.int32, (C, W), 1)

    def put(buf, row, x):
        buf[pl.ds(row * 3 * C, C), :] = jnp.where(lane == 0, 0.0, pltpu.roll(x, 1, 1)).astype(jnp.bfloat16)
        buf[pl.ds(row * 3 * C + C, C), :] = x.astype(jnp.bfloat16)
        buf[pl.ds(row * 3 * C + 2 * C, C), :] = jnp.where(lane == W - 1, 0.0, pltpu.roll(x, W - 1, 1)).astype(jnp.bfloat16)

    upf, downf = up.astype(jnp.float32), down.astype(jnp.float32)

    def arrive(r):
        if r == 0:
            @pl.when(up)
            def _():
                to_down.wait_recv()

            @pl.when(jnp.logical_not(up))
            def _():
                ext[pl.ds(0, H * C), :] = jnp.zeros((H * C, W), jnp.bfloat16)
        elif r == R + H:
            @pl.when(down)
            def _():
                to_up.wait_recv()

            @pl.when(jnp.logical_not(down))
            def _():
                ext[pl.ds((R + H) * C, H * C), :] = jnp.zeros((H * C, W), jnp.bfloat16)
        elif H <= r < R + H and (r - H) % PR == 0:
            main[(r - H) // PR].wait_recv()
        x = ext[pl.ds(r * C, C), :].astype(jnp.float32)
        put(ha, r, x)
        if H <= r < R + H:
            guess[pl.ds((r - H) * C, C), :] = jnp.where(t == 0, start_r[pl.ds((r - H) * C, C), :], x)

    src, dst = ha, hbuf
    wide = (Q + 2) * 3 * C

    def gather(buf, first, count):
        parts = []
        for i in range(count):
            at = (first + Q * i) * 3 * C
            parts.append(buf[pl.ds(at if isinstance(at, int) else pl.multiple_of(at, 3 * C), wide), :])
        return jnp.concatenate(parts, axis=1)

    here = 0
    for l in range(layers):
        rows = R + 2 * (H - 1 - l)
        edge = H - 1 - l
        pairs = rows // Q
        for lo in range(0, pairs, 2):
            count = min(2, pairs - lo)
            if l == 0:
                while here < Q * (lo + count) + 2:
                    arrive(here)
                    here += 1
            o = jnp.dot(wh[l], gather(src, Q * lo, count), preferred_element_type=jnp.float32)
            for i in range(count):
                for q in range(Q):
                    row = Q * (lo + i) + q
                    pre = o[q * C:(q + 1) * C, i * W:(i + 1) * W] + biases[l]
                    h = pre * jax.nn.sigmoid(pre)
                    if row < edge:
                        h = h * upf
                    elif row >= R + edge:
                        h = h * downf
                    put(dst, row, h)
        src, dst = dst, src

    def ab_copy(p, j):
        return pltpu.make_async_remote_copy(
            src_ref=ab.at[j], dst_ref=rab.at[m], send_sem=s_ab.at[p], recv_sem=r_ab.at[p],
            device_id=(base + j, s), device_id_type=MESH)

    acc = jnp.zeros((C, W), jnp.float32)
    for p in range(1, G + 1):
        j = lax.rem(m + p, G)
        for lo in range(0, RG // Q, 2):
            count = min(2, RG // Q - lo)
            o = jnp.dot(wo[...], gather(src, j * RG + Q * lo, count), preferred_element_type=jnp.float32)
            for i in range(count):
                for q in range(Q):
                    own = Q * (lo + i) + q
                    row = j * RG + own
                    hd = o[q * 2 * C:(q + 1) * 2 * C, i * W:(i + 1) * W]
                    x = guess[pl.ds(pl.multiple_of(row * C, C), C), :]
                    cand = jnp.tanh(hd[:C] + cb + skip * x)
                    gate = jax.nn.sigmoid(hd[C:] + gb)
                    f = gate * x + (1.0 - gate) * cand
                    jac = gate + (1.0 - gate) * (1.0 - cand * cand) * skip
                    d = traj[pl.ds(row, C, stride=R), :] - f
                    acc = acc + d * d
                    ab[j, 0, pl.ds(own * C, C), :] = jac
                    ab[j, 1, pl.ds(own * C, C), :] = f - jac * x
        if p < G:
            ab_copy(p, j).start()
    rab[m] = ab[m]
    part[...] = jnp.sum(acc.reshape(C // 8, 8, W), axis=0)

    def ps_copy(p):
        return pltpu.make_async_remote_copy(
            src_ref=part, dst_ref=rpart.at[p - 1], send_sem=s_ps.at[p - 1], recv_sem=r_ps.at[p - 1],
            device_id=(t, lax.rem(s + p, S)), device_id_type=MESH)

    for p in range(1, S):
        ps_copy(p).start()
    for p in range(1, G):
        ab_copy(p, lax.rem(m + p, G)).wait_recv()

    def chain(k):
        return pltpu.make_async_remote_copy(
            src_ref=cout.at[k], dst_ref=cin.at[k], send_sem=s_ch.at[k], recv_sem=r_ch.at[k],
            device_id=(lax.rem(t + G, T), s), device_id_type=MESH)

    def st_copy(p, k):
        j = lax.rem(m + p, G)
        return pltpu.make_async_remote_copy(
            src_ref=ys.at[j, k], dst_ref=st.at[m, k], send_sem=s_st.at[p, k], recv_sem=r_st.at[p, k],
            device_id=(base + j, s), device_id_type=MESH)

    for k in range(K):
        @pl.when(g == 0)
        def _():
            cin[k] = start_r[pl.ds(m * L + k * CH, CH), :]

        @pl.when(g > 0)
        def _():
            chain(k).wait_recv()

        y = cin[k]
        for j in range(G):
            ys[j, k] = y
            y = rab[j, 0, pl.ds(k * CH, CH), :] * y + rab[j, 1, pl.ds(k * CH, CH), :]
        cout[k] = y

        @pl.when(g < NG - 1)
        def _():
            chain(k).start()

        @pl.when(g == NG - 1)
        def _():
            for p in range(1, G):
                st_copy(p, k).start()

    @pl.when(g < NG - 1)
    def _():
        for k in range(K):
            for p in range(1, G):
                st_copy(p, k).start()

    total = part[...]
    for p in range(1, S):
        ps_copy(p).wait_recv()
        total = total + rpart[p - 1]
    res[0] = jnp.sum(total) * (1.0 / (C * R * S * W))

    for k in range(K):
        for p in range(G):
            j = lax.rem(m + G - p, G)
            if p > 0:
                st_copy(p, k).wait_recv()
                y = st[j, k]
            else:
                y = ys[m, k]
            for i in range(CH // C):
                own = k * (CH // C) + i
                out[pl.ds(j * RG + own, C, stride=R), :] = (
                    ab[j, 0, pl.ds(own * C, C), :] * y[i * C:(i + 1) * C] + ab[j, 1, pl.ds(own * C, C), :])

    for copy in main:
        copy.wait_send()

    @pl.when(down)
    def _():
        to_down.wait_send()

    @pl.when(up)
    def _():
        to_up.wait_send()

    for p in range(1, S):
        ps_copy(p).wait_send()
    for p in range(1, G):
        ab_copy(p, lax.rem(m + p, G)).wait_send()
        for k in range(K):
            st_copy(p, k).wait_send()

    @pl.when(g < NG - 1)
    def _():
        for k in range(K):
            chain(k).wait_send()


def group_of(T, R):
    best = 1
    for n in range(1, T + 1):
        if T % n == 0 and R % n == 0 and n * n <= T:
            best = n
    return best


def body(T, S, traj, start, actions, hw, hb, headw, cand_b, gate_b, skip, proj):
    steps, C, R, W = traj.shape
    layers = hw.shape[0]
    G = group_of(T, R)
    K = R // G
    H = layers + 1
    L = R * C // G
    CH = L // K
    f32, bf16 = jnp.float32, jnp.bfloat16
    wide = (Q + 2) * 3 * C
    DMA = pltpu.SemaphoreType.DMA
    spec = pl.BlockSpec(memory_space=VMEM)
    new, res = pl.pallas_call(
        functools.partial(kernel, T, S, G, K, C, R, W, layers),
        out_shape=(jax.ShapeDtypeStruct((C * R, W), f32), jax.ShapeDtypeStruct((1,), f32)),
        in_specs=[pl.BlockSpec(memory_space=pltpu.HBM)] * 2 + [spec] * 8,
        out_specs=(spec, pl.BlockSpec(memory_space=pltpu.SMEM)),
        scratch_shapes=[
            VMEM((C * R, W), f32),
            VMEM((C * R, W), f32),
            VMEM((R * C, W), bf16),
            VMEM(((R + 2 * H) * C, W), bf16),
            VMEM(((R + 2 * H) * 3 * C, W), bf16),
            VMEM(((R + 2 * H) * 3 * C, W), bf16),
            VMEM((layers, Q * C, wide), bf16),
            VMEM((Q * 2 * C, wide), bf16),
            VMEM((R * C, W), f32),
            VMEM((R * C, W), f32),
            VMEM((G, 2, L, W), f32),
            VMEM((G, 2, L, W), f32),
            VMEM((K, CH, W), f32),
            VMEM((K, CH, W), f32),
            VMEM((G, K, CH, W), f32),
            VMEM((G, K, CH, W), f32),
            VMEM((8, W), f32),
            VMEM((max(S - 1, 1), 8, W), f32),
            DMA((2,)),
            DMA((2 + PARTS,)), DMA((2 + PARTS,)),
            DMA((G,)), DMA((G,)),
            DMA((K,)), DMA((K,)),
            DMA((G, K)), DMA((G, K)),
            DMA((max(S - 1, 1),)), DMA((max(S - 1, 1),)),
        ],
        compiler_params=pltpu.CompilerParams(
            collective_id=0, has_side_effects=True, vmem_limit_bytes=63 * 1024 * 1024),
    )(
        traj.reshape(C * R, W), start.reshape(C * R, W), actions,
        hw.reshape(-1, hw.shape[-1]), hb, headw.swapaxes(1, 2).reshape(-1, headw.shape[1]),
        cand_b.reshape(1, C), gate_b.reshape(1, C), skip.reshape(1, C), proj,
    )
    return new.reshape(traj.shape), res


def solution(mesh):
    return jax.shard_map(
        functools.partial(body, mesh.shape["tm"], mesh.shape["space"]),
        mesh=mesh,
        in_specs=(
            P("tm", None, "space", None),
            P(None, "space", None),
            P("tm", None),
            P(), P(), P(), P(), P(), P(), P(),
        ),
        out_specs=(P("tm", None, "space", None), P("tm")),
        check_vma=False,
    )
```

```python
import functools

import jax
import jax.numpy as jnp
from jax import lax
from jax.experimental import pallas as pl
from jax.experimental.pallas import tpu as pltpu
from jax.sharding import PartitionSpec as P

MESH = pl.DeviceIdType.MESH
Q = 2
VMEM = pltpu.VMEM


def column(row):
    n = row.shape[1]
    eye = lax.broadcasted_iota(jnp.int32, (n, n), 0) == lax.broadcasted_iota(jnp.int32, (n, n), 1)
    return jnp.sum(jnp.where(eye, jnp.broadcast_to(row, (n, n)), 0.0), axis=1, keepdims=True)


def kernel(
    T, S, G, K, C, R, W, layers,
    traj_h, start_h, actions, hw, hb, headw, cand_b, gate_b, skip_r, proj,
    out, res,
    traj, start, sendb, ext, tnext, actn, f0, ha, hbuf, wh, wo, guess, ab, rab, cin, cout, ys, st, part, rpart,
    s_in, s_prior, r_prior, s_ab, r_ab, s_ch, r_ch, s_st, r_st, s_ps, r_ps, s_f0, r_f0,
):
    H = layers + 1
    L = R * C // G
    CH = L // K
    per = CH // C
    NG = T // G
    RG = R // G
    t = lax.axis_index("tm")
    s = lax.axis_index("space")
    g = t // G
    m = lax.rem(t, G)
    base = g * G
    nxt, prv = lax.rem(t + 1, T), lax.rem(t + T - 1, T)
    peers = []
    for tt in (nxt, prv):
        for ds in range(S):
            peers.append((tt, lax.rem(s + ds, S)))
    for p in range(1, G):
        peers.append((base + lax.rem(m + p, G), s))
    for step in (G, T - G):
        if NG > 1:
            peers.append((lax.rem(t + step, T), s))
    for p in range(1, S):
        peers.append((t, lax.rem(s + p, S)))
    load_t = pltpu.make_async_copy(traj_h, traj, s_in.at[0])
    load_s = pltpu.make_async_copy(start_h, start, s_in.at[1])
    load_t.start()
    load_s.start()
    barrier = pltpu.get_barrier_semaphore()
    last = t == T - 1
    early = t < G
    for peer in peers:
        pl.semaphore_signal(barrier, inc=1, device_id=peer, device_id_type=MESH)


    @pl.when(early)
    def _():
        pl.semaphore_signal(barrier, inc=1, device_id=(T - 1, s), device_id_type=MESH)

    @pl.when(last)
    def _():
        for j in range(G):
            pl.semaphore_signal(barrier, inc=1, device_id=(j, s), device_id_type=MESH)

    wh[...] = jnp.zeros_like(wh)
    wo[...] = jnp.zeros_like(wo)
    taps = [headw[pl.ds(k * C, C), :].astype(jnp.float32).T.astype(jnp.bfloat16) for k in range(9)]
    for q in range(Q):
        for a in range(3):
            for b in range(3):
                at = ((q + a) * 3 + b) * C
                for l in range(layers):
                    wh[l, pl.ds(q * C, C), pl.ds(at, C)] = hw[pl.ds((l * 9 + 3 * a + b) * C, C), :]
                wo[pl.ds(q * 2 * C, 2 * C), pl.ds(at, C)] = taps[3 * a + b]
    load_t.wait()
    load_s.wait()
    for r in range(R):
        row = traj[pl.ds(r, C, stride=R), :]
        x = jnp.where(last, start[pl.ds(r, C, stride=R), :], row)
        guess[pl.ds(r * C, C), :] = x
        ext[pl.ds((H + r) * C, C), :] = x.astype(jnp.bfloat16)
        sendb[pl.ds(r * C, C), :] = row.astype(jnp.bfloat16)

    pl.semaphore_wait(barrier, len(peers) + early.astype(jnp.int32) + G * last.astype(jnp.int32))

    def prior_copy(i, src, dst, to):
        return pltpu.make_async_remote_copy(
            src_ref=src, dst_ref=dst, send_sem=s_prior.at[i], recv_sem=r_prior.at[i],
            device_id=to, device_id_type=MESH)

    up, down = s > 0, s < S - 1
    to_down = prior_copy(0, ext.at[pl.ds(R * C, H * C)], ext.at[pl.ds(0, H * C)], (t, lax.rem(s + 1, S)))
    to_up = prior_copy(1, ext.at[pl.ds(H * C, H * C)], ext.at[pl.ds((R + H) * C, H * C)], (t, lax.rem(s + S - 1, S)))
    act_copy = prior_copy(2, actions, actn, (prv, s))
    main = prior_copy(3, sendb, tnext, (prv, s))
    act_copy.start()

    @pl.when(down)
    def _():
        to_down.start()

    @pl.when(up)
    def _():
        to_up.start()

    main.start()
    act_copy.wait_recv()
    act = column(jnp.sum(column(actn[...]) * proj[...], axis=0, keepdims=True))
    biases = [column(hb[pl.ds(l, 1), :]) for l in range(layers)]
    biases[0] = biases[0] + act[:C]
    cb = column(cand_b[...])
    gb = column(gate_b[...]) + act[C:]
    skip = column(skip_r[...])
    lane = lax.broadcasted_iota(jnp.int32, (C, W), 1)

    def put(buf, row, x):
        buf[pl.ds(row * 3 * C, C), :] = jnp.where(lane == 0, 0.0, pltpu.roll(x, 1, 1)).astype(jnp.bfloat16)
        buf[pl.ds(row * 3 * C + C, C), :] = x.astype(jnp.bfloat16)
        buf[pl.ds(row * 3 * C + 2 * C, C), :] = jnp.where(lane == W - 1, 0.0, pltpu.roll(x, W - 1, 1)).astype(jnp.bfloat16)

    upf, downf = up.astype(jnp.float32), down.astype(jnp.float32)

    def arrive(r):
        if r == 0:
            @pl.when(up)
            def _():
                to_down.wait_recv()

            @pl.when(jnp.logical_not(up))
            def _():
                ext[pl.ds(0, H * C), :] = jnp.zeros((H * C, W), jnp.bfloat16)
        elif r == R + H:
            @pl.when(down)
            def _():
                to_up.wait_recv()

            @pl.when(jnp.logical_not(down))
            def _():
                ext[pl.ds((R + H) * C, H * C), :] = jnp.zeros((H * C, W), jnp.bfloat16)
        x = ext[pl.ds(r * C, C), :].astype(jnp.float32)
        put(ha, r, x)

    src, dst = ha, hbuf
    wide = (Q + 2) * 3 * C

    def gather(buf, first, count):
        parts = []
        for i in range(count):
            at = (first + Q * i) * 3 * C
            parts.append(buf[pl.ds(at if isinstance(at, int) else pl.multiple_of(at, 3 * C), wide), :])
        return jnp.concatenate(parts, axis=1)

    here = 0
    for l in range(layers):
        rows = R + 2 * (H - 1 - l)
        edge = H - 1 - l
        pairs = rows // Q
        for lo in range(0, pairs, 2):
            count = min(2, pairs - lo)
            if l == 0:
                while here < Q * (lo + count) + 2:
                    arrive(here)
                    here += 1
            o = jnp.dot(wh[l], gather(src, Q * lo, count), preferred_element_type=jnp.float32)
            for i in range(count):
                for q in range(Q):
                    row = Q * (lo + i) + q
                    pre = o[q * C:(q + 1) * C, i * W:(i + 1) * W] + biases[l]
                    h = pre * jax.nn.sigmoid(pre)
                    if row < edge:
                        h = h * upf
                    elif row >= R + edge:
                        h = h * downf
                    put(dst, row, h)
        src, dst = dst, src

    def ab_copy(p, j):
        return pltpu.make_async_remote_copy(
            src_ref=ab.at[j], dst_ref=rab.at[m], send_sem=s_ab.at[p], recv_sem=r_ab.at[p],
            device_id=(base + j, s), device_id_type=MESH)

    def f0_copy(j):
        return pltpu.make_async_remote_copy(
            src_ref=f0.at[j], dst_ref=cin, send_sem=s_f0.at[j], recv_sem=r_f0.at[0],
            device_id=(j, s), device_id_type=MESH)

    main.wait_recv()
    acc = jnp.zeros((C, W), jnp.float32)
    for p in range(1, G + 1):
        j = lax.rem(m + p, G)
        for lo in range(0, RG // Q, 2):
            count = min(2, RG // Q - lo)
            o = jnp.dot(wo[...], gather(src, j * RG + Q * lo, count), preferred_element_type=jnp.float32)
            for i in range(count):
                for q in range(Q):
                    own = Q * (lo + i) + q
                    row = j * RG + own
                    hd = o[q * 2 * C:(q + 1) * 2 * C, i * W:(i + 1) * W]
                    x = guess[pl.ds(pl.multiple_of(row * C, C), C), :]
                    cand = jnp.tanh(hd[:C] + cb + skip * x)
                    gate = jax.nn.sigmoid(hd[C:] + gb)
                    f = gate * x + (1.0 - gate) * cand
                    jac = gate + (1.0 - gate) * (1.0 - cand * cand) * skip
                    d = tnext[pl.ds(pl.multiple_of(row * C, C), C), :].astype(jnp.float32) - f
                    acc = acc + d * d
                    ab[j, 0, pl.ds(own * C, C), :] = jac
                    ab[j, 1, pl.ds(own * C, C), :] = f - jac * x
                    f0[j, own // per, pl.ds((own % per) * C, C), :] = f
        @pl.when(last)
        def _():
            f0_copy(j).start()

        if p < G:
            ab_copy(p, j).start()
    rab[m] = ab[m]
    part[...] = jnp.sum(acc.reshape(C // 8, 8, W), axis=0)

    def ps_copy(p):
        return pltpu.make_async_remote_copy(
            src_ref=part, dst_ref=rpart.at[p], send_sem=s_ps.at[p], recv_sem=r_ps.at[p],
            device_id=(nxt, lax.rem(s + p, S)), device_id_type=MESH)

    for p in range(S):
        ps_copy(p).start()
    for p in range(1, G):
        ab_copy(p, lax.rem(m + p, G)).wait_recv()

    def chain(k):
        return pltpu.make_async_remote_copy(
            src_ref=cout.at[k], dst_ref=cin.at[k], send_sem=s_ch.at[k], recv_sem=r_ch.at[k],
            device_id=(lax.rem(t + G, T), s), device_id_type=MESH)

    def st_copy(p, k):
        j = lax.rem(m + p, G)
        return pltpu.make_async_remote_copy(
            src_ref=ys.at[j, k], dst_ref=st.at[m, k], send_sem=s_st.at[p, k], recv_sem=r_st.at[p, k],
            device_id=(base + j, s), device_id_type=MESH)

    @pl.when(early)
    def _():
        f0_copy(t).wait_recv()

    for k in range(K):
        @pl.when(g > 0)
        def _():
            chain(k).wait_recv()

        y = cin[k]
        for j in range(G):
            ys[j, k] = y
            y = rab[j, 0, pl.ds(k * CH, CH), :] * y + rab[j, 1, pl.ds(k * CH, CH), :]
        cout[k] = y

        @pl.when(g < NG - 1)
        def _():
            chain(k).start()

        @pl.when(g == NG - 1)
        def _():
            for p in range(1, G):
                st_copy(p, k).start()

    @pl.when(g < NG - 1)
    def _():
        for k in range(K):
            for p in range(1, G):
                st_copy(p, k).start()

    total = jnp.zeros((8, W), jnp.float32)
    for p in range(S):
        ps_copy(p).wait_recv()
        total = total + rpart[p]
    res[0] = jnp.sum(total) * (1.0 / (C * R * S * W))

    for k in range(K):
        for p in range(G):
            j = lax.rem(m + G - p, G)
            if p > 0:
                st_copy(p, k).wait_recv()
                y = st[j, k]
            else:
                y = ys[m, k]
            for i in range(CH // C):
                own = k * (CH // C) + i
                out[pl.ds(j * RG + own, C, stride=R), :] = y[i * C:(i + 1) * C]

    main.wait_send()
    act_copy.wait_send()

    @pl.when(last)
    def _():
        for j in range(G):
            f0_copy(j).wait_send()

    @pl.when(down)
    def _():
        to_down.wait_send()

    @pl.when(up)
    def _():
        to_up.wait_send()

    for p in range(S):
        ps_copy(p).wait_send()
    for p in range(1, G):
        ab_copy(p, lax.rem(m + p, G)).wait_send()
        for k in range(K):
            st_copy(p, k).wait_send()

    @pl.when(g < NG - 1)
    def _():
        for k in range(K):
            chain(k).wait_send()


def group_of(T, R):
    best = 1
    for n in range(1, T + 1):
        if T % n == 0 and R % n == 0 and n * n <= T:
            best = n
    return best


def body(T, S, traj, start, actions, hw, hb, headw, cand_b, gate_b, skip, proj):
    steps, C, R, W = traj.shape
    layers = hw.shape[0]
    G = group_of(T, R)
    K = R // G
    H = layers + 1
    L = R * C // G
    CH = L // K
    f32, bf16 = jnp.float32, jnp.bfloat16
    wide = (Q + 2) * 3 * C
    DMA = pltpu.SemaphoreType.DMA
    spec = pl.BlockSpec(memory_space=VMEM)
    new, res = pl.pallas_call(
        functools.partial(kernel, T, S, G, K, C, R, W, layers),
        out_shape=(VMEM((C * R, W), f32), jax.ShapeDtypeStruct((1,), f32)),
        in_specs=[pl.BlockSpec(memory_space=pltpu.HBM)] * 2 + [spec] * 8,
        out_specs=(spec, pl.BlockSpec(memory_space=pltpu.SMEM)),
        scratch_shapes=[
            VMEM((C * R, W), f32),
            VMEM((C * R, W), f32),
            VMEM((R * C, W), bf16),
            VMEM(((R + 2 * H) * C, W), bf16),
            VMEM((R * C, W), bf16),
            VMEM(actions.shape, f32),
            VMEM((G, K, CH, W), f32),
            VMEM(((R + 2 * H) * 3 * C, W), bf16),
            VMEM(((R + 2 * H) * 3 * C, W), bf16),
            VMEM((layers, Q * C, wide), bf16),
            VMEM((Q * 2 * C, wide), bf16),
            VMEM((R * C, W), f32),
            VMEM((G, 2, L, W), f32),
            VMEM((G, 2, L, W), f32),
            VMEM((K, CH, W), f32),
            VMEM((K, CH, W), f32),
            VMEM((G, K, CH, W), f32),
            VMEM((G, K, CH, W), f32),
            VMEM((8, W), f32),
            VMEM((S, 8, W), f32),
            DMA((2,)),
            DMA((4,)), DMA((4,)),
            DMA((G,)), DMA((G,)),
            DMA((K,)), DMA((K,)),
            DMA((G, K)), DMA((G, K)),
            DMA((S,)), DMA((S,)),
            DMA((G,)), DMA((1,)),
        ],
        compiler_params=pltpu.CompilerParams(
            collective_id=0, has_side_effects=True, vmem_limit_bytes=63 * 1024 * 1024),
    )(
        traj.reshape(C * R, W), start.reshape(C * R, W), actions,
        hw.reshape(-1, hw.shape[-1]), hb, headw.swapaxes(1, 2).reshape(-1, headw.shape[1]),
        cand_b.reshape(1, C), gate_b.reshape(1, C), skip.reshape(1, C), proj,
    )
    return new.reshape(traj.shape), res


def solution(mesh):
    return jax.shard_map(
        functools.partial(body, mesh.shape["tm"], mesh.shape["space"]),
        mesh=mesh,
        in_specs=(
            P("tm", None, "space", None),
            P(None, "space", None),
            P("tm", None),
            P(), P(), P(), P(), P(), P(), P(),
        ),
        out_specs=(P("tm", None, "space", None), P("tm")),
        check_vma=False,
    )
```

```python
import functools

import jax
import jax.numpy as jnp
from jax import lax
from jax.experimental import pallas as pl
from jax.experimental.pallas import tpu as pltpu
from jax.sharding import PartitionSpec as P

MESH = pl.DeviceIdType.MESH
Q = 2
VMEM = pltpu.VMEM


def column(row):
    n = row.shape[1]
    eye = lax.broadcasted_iota(jnp.int32, (n, n), 0) == lax.broadcasted_iota(jnp.int32, (n, n), 1)
    return jnp.sum(jnp.where(eye, jnp.broadcast_to(row, (n, n)), 0.0), axis=1, keepdims=True)


def kernel(
    T, S, G, K, C, R, W, layers,
    traj_h, start_h, actions, hw, hb, headw, cand_b, gate_b, skip_r, proj,
    out, res,
    traj, start, sendb, ext, tnext, actn, f0, ha, hbuf, wh, wo, guess, ab, rab, cin, cout, ys, st, part, rpart,
    s_in, s_prior, r_prior, s_ab, r_ab, s_ch, r_ch, s_st, r_st, s_ps, r_ps, s_f0, r_f0,
):
    H = layers + 1
    L = R * C // G
    CH = L // K
    per = CH // C
    NG = T // G
    RG = R // G
    t = lax.axis_index("tm")
    s = lax.axis_index("space")
    g = t // G
    m = lax.rem(t, G)
    base = g * G
    nxt, prv = lax.rem(t + 1, T), lax.rem(t + T - 1, T)
    peers = []
    for tt in (nxt, prv):
        for ds in range(S):
            peers.append((tt, lax.rem(s + ds, S)))
    for p in range(1, G):
        peers.append((base + lax.rem(m + p, G), s))
    for step in (G, T - G):
        if NG > 1:
            peers.append((lax.rem(t + step, T), s))
    for p in range(1, S):
        peers.append((t, lax.rem(s + p, S)))
    load_t = pltpu.make_async_copy(traj_h, traj, s_in.at[0])
    load_s = pltpu.make_async_copy(start_h, start, s_in.at[1])
    load_t.start()
    load_s.start()
    barrier = pltpu.get_barrier_semaphore()
    last = t == T - 1
    early = t < G
    for peer in peers:
        pl.semaphore_signal(barrier, inc=1, device_id=peer, device_id_type=MESH)


    @pl.when(early)
    def _():
        pl.semaphore_signal(barrier, inc=1, device_id=(T - 1, s), device_id_type=MESH)

    @pl.when(last)
    def _():
        for j in range(G):
            pl.semaphore_signal(barrier, inc=1, device_id=(j, s), device_id_type=MESH)

    wh[...] = jnp.zeros_like(wh)
    wo[...] = jnp.zeros_like(wo)
    taps = [headw[pl.ds(k * C, C), :].astype(jnp.float32).T.astype(jnp.bfloat16) for k in range(9)]
    for q in range(Q):
        for a in range(3):
            for b in range(3):
                at = ((q + a) * 3 + b) * C
                for l in range(layers):
                    wh[l, pl.ds(q * C, C), pl.ds(at, C)] = hw[pl.ds((l * 9 + 3 * a + b) * C, C), :]
                wo[pl.ds(q * 2 * C, 2 * C), pl.ds(at, C)] = taps[3 * a + b]
    load_t.wait()
    load_s.wait()
    for r in range(R):
        row = traj[pl.ds(r, C, stride=R), :]
        x = jnp.where(last, start[pl.ds(r, C, stride=R), :], row)
        guess[pl.ds(r * C, C), :] = x
        ext[pl.ds((H + r) * C, C), :] = x.astype(jnp.bfloat16)
        sendb[pl.ds(r * C, C), :] = row.astype(jnp.bfloat16)

    pl.semaphore_wait(barrier, len(peers) + early.astype(jnp.int32) + G * last.astype(jnp.int32))

    def prior_copy(i, src, dst, to):
        return pltpu.make_async_remote_copy(
            src_ref=src, dst_ref=dst, send_sem=s_prior.at[i], recv_sem=r_prior.at[i],
            device_id=to, device_id_type=MESH)

    up, down = s > 0, s < S - 1
    to_down = prior_copy(0, ext.at[pl.ds(R * C, H * C)], ext.at[pl.ds(0, H * C)], (t, lax.rem(s + 1, S)))
    to_up = prior_copy(1, ext.at[pl.ds(H * C, H * C)], ext.at[pl.ds((R + H) * C, H * C)], (t, lax.rem(s + S - 1, S)))
    act_copy = prior_copy(2, actions, actn, (prv, s))
    main = prior_copy(3, sendb, tnext, (prv, s))
    act_copy.start()

    @pl.when(down)
    def _():
        to_down.start()

    @pl.when(up)
    def _():
        to_up.start()

    main.start()
    act_copy.wait_recv()
    act = column(jnp.sum(column(actn[...]) * proj[...], axis=0, keepdims=True))
    biases = [column(hb[pl.ds(l, 1), :]) for l in range(layers)]
    biases[0] = biases[0] + act[:C]
    cb = column(cand_b[...])
    gb = column(gate_b[...]) + act[C:]
    skip = column(skip_r[...])
    lane = lax.broadcasted_iota(jnp.int32, (C, W), 1)

    def put(buf, row, x):
        buf[pl.ds(row * 3 * C, C), :] = jnp.where(lane == 0, 0.0, pltpu.roll(x, 1, 1)).astype(jnp.bfloat16)
        buf[pl.ds(row * 3 * C + C, C), :] = x.astype(jnp.bfloat16)
        buf[pl.ds(row * 3 * C + 2 * C, C), :] = jnp.where(lane == W - 1, 0.0, pltpu.roll(x, W - 1, 1)).astype(jnp.bfloat16)

    upf, downf = up.astype(jnp.float32), down.astype(jnp.float32)

    def arrive(r):
        if r == 0:
            @pl.when(up)
            def _():
                to_down.wait_recv()

            @pl.when(jnp.logical_not(up))
            def _():
                ext[pl.ds(0, H * C), :] = jnp.zeros((H * C, W), jnp.bfloat16)
        elif r == R + H:
            @pl.when(down)
            def _():
                to_up.wait_recv()

            @pl.when(jnp.logical_not(down))
            def _():
                ext[pl.ds((R + H) * C, H * C), :] = jnp.zeros((H * C, W), jnp.bfloat16)
        x = ext[pl.ds(r * C, C), :].astype(jnp.float32)
        put(ha, r, x)

    src, dst = ha, hbuf
    wide = (Q + 2) * 3 * C

    def gather(buf, first, count):
        parts = []
        for i in range(count):
            at = (first + Q * i) * 3 * C
            parts.append(buf[pl.ds(at if isinstance(at, int) else pl.multiple_of(at, 3 * C), wide), :])
        return jnp.concatenate(parts, axis=1)

    here = 0
    for l in range(layers):
        rows = R + 2 * (H - 1 - l)
        edge = H - 1 - l
        pairs = rows // Q
        for lo in range(0, pairs, 2):
            count = min(2, pairs - lo)
            if l == 0:
                while here < Q * (lo + count) + 2:
                    arrive(here)
                    here += 1
            o = jnp.dot(wh[l], gather(src, Q * lo, count), preferred_element_type=jnp.float32)
            for i in range(count):
                for q in range(Q):
                    row = Q * (lo + i) + q
                    pre = o[q * C:(q + 1) * C, i * W:(i + 1) * W] + biases[l]
                    h = pre * jax.nn.sigmoid(pre)
                    if row < edge:
                        h = h * upf
                    elif row >= R + edge:
                        h = h * downf
                    put(dst, row, h)
        src, dst = dst, src

    def ab_copy(p, j):
        return pltpu.make_async_remote_copy(
            src_ref=ab.at[j], dst_ref=rab.at[m], send_sem=s_ab.at[p], recv_sem=r_ab.at[p],
            device_id=(base + j, s), device_id_type=MESH)

    def f0_copy(j):
        return pltpu.make_async_remote_copy(
            src_ref=f0.at[j], dst_ref=cin, send_sem=s_f0.at[j], recv_sem=r_f0.at[0],
            device_id=(j, s), device_id_type=MESH)

    main.wait_recv()
    acc = jnp.zeros((C, W), jnp.float32)
    for p in range(1, G + 1):
        j = lax.rem(m + p, G)
        for lo in range(0, RG // Q, 2):
            count = min(2, RG // Q - lo)
            o = jnp.dot(wo[...], gather(src, j * RG + Q * lo, count), preferred_element_type=jnp.float32)
            for i in range(count):
                for q in range(Q):
                    own = Q * (lo + i) + q
                    row = j * RG + own
                    hd = o[q * 2 * C:(q + 1) * 2 * C, i * W:(i + 1) * W]
                    x = guess[pl.ds(pl.multiple_of(row * C, C), C), :]
                    cand = jnp.tanh(hd[:C] + cb + skip * x)
                    gate = jax.nn.sigmoid(hd[C:] + gb)
                    f = gate * x + (1.0 - gate) * cand
                    jac = gate + (1.0 - gate) * (1.0 - cand * cand) * skip
                    d = tnext[pl.ds(pl.multiple_of(row * C, C), C), :].astype(jnp.float32) - f
                    acc = acc + d * d
                    ab[j, 0, pl.ds(own * C, C), :] = jac
                    ab[j, 1, pl.ds(own * C, C), :] = f - jac * x
                    f0[j, own // per, pl.ds((own % per) * C, C), :] = f
        @pl.when(last)
        def _():
            f0_copy(j).start()

        if p < G:
            @pl.when(jnp.logical_not(last))
            def _():
                ab_copy(p, j).start()
    rab[m] = ab[m]
    part[...] = jnp.sum(acc.reshape(C // 8, 8, W), axis=0)

    def ps_copy(p):
        return pltpu.make_async_remote_copy(
            src_ref=part, dst_ref=rpart.at[p], send_sem=s_ps.at[p], recv_sem=r_ps.at[p],
            device_id=(nxt, lax.rem(s + p, S)), device_id_type=MESH)

    for p in range(S):
        ps_copy(p).start()
    for p in range(1, G):
        @pl.when(base + lax.rem(m + G - p, G) != T - 1)
        def _():
            ab_copy(p, lax.rem(m + p, G)).wait_recv()


    def chain(k):
        return pltpu.make_async_remote_copy(
            src_ref=cout.at[k], dst_ref=cin.at[k], send_sem=s_ch.at[k], recv_sem=r_ch.at[k],
            device_id=(lax.rem(t + G, T), s), device_id_type=MESH)

    def st_copy(p, k):
        j = lax.rem(m + p, G)
        return pltpu.make_async_remote_copy(
            src_ref=ys.at[j, k], dst_ref=st.at[m, k], send_sem=s_st.at[p, k], recv_sem=r_st.at[p, k],
            device_id=(base + j, s), device_id_type=MESH)

    @pl.when(early)
    def _():
        f0_copy(t).wait_recv()

    for k in range(K):
        @pl.when(g > 0)
        def _():
            chain(k).wait_recv()

        y = cin[k]
        for j in range(G):
            ys[j, k] = y
            y = rab[j, 0, pl.ds(k * CH, CH), :] * y + rab[j, 1, pl.ds(k * CH, CH), :]
        cout[k] = y

        @pl.when(g < NG - 1)
        def _():
            chain(k).start()

        @pl.when(g == NG - 1)
        def _():
            for p in range(1, G):
                st_copy(p, k).start()

    @pl.when(g < NG - 1)
    def _():
        for k in range(K):
            for p in range(1, G):
                st_copy(p, k).start()

    total = jnp.zeros((8, W), jnp.float32)
    for p in range(S):
        ps_copy(p).wait_recv()
        total = total + rpart[p]
    res[0] = jnp.sum(total) * (1.0 / (C * R * S * W))

    for k in range(K):
        for p in range(G):
            j = lax.rem(m + G - p, G)
            if p > 0:
                st_copy(p, k).wait_recv()
                y = st[j, k]
            else:
                y = ys[m, k]
            for i in range(CH // C):
                own = k * (CH // C) + i
                out[pl.ds(j * RG + own, C, stride=R), :] = y[i * C:(i + 1) * C]

    main.wait_send()
    act_copy.wait_send()

    @pl.when(last)
    def _():
        for j in range(G):
            f0_copy(j).wait_send()

    @pl.when(down)
    def _():
        to_down.wait_send()

    @pl.when(up)
    def _():
        to_up.wait_send()

    for p in range(S):
        ps_copy(p).wait_send()
    for p in range(1, G):
        @pl.when(jnp.logical_not(last))
        def _():
            ab_copy(p, lax.rem(m + p, G)).wait_send()

        for k in range(K):
            st_copy(p, k).wait_send()

    @pl.when(g < NG - 1)
    def _():
        for k in range(K):
            chain(k).wait_send()


def group_of(T, R):
    best = 1
    for n in range(1, T + 1):
        if T % n == 0 and R % n == 0 and n * n <= T:
            best = n
    return best


def body(T, S, traj, start, actions, hw, hb, headw, cand_b, gate_b, skip, proj):
    steps, C, R, W = traj.shape
    layers = hw.shape[0]
    G = group_of(T, R)
    K = R // G
    H = layers + 1
    L = R * C // G
    CH = L // K
    f32, bf16 = jnp.float32, jnp.bfloat16
    wide = (Q + 2) * 3 * C
    DMA = pltpu.SemaphoreType.DMA
    spec = pl.BlockSpec(memory_space=VMEM)
    new, res = pl.pallas_call(
        functools.partial(kernel, T, S, G, K, C, R, W, layers),
        out_shape=(VMEM((C * R, W), f32), jax.ShapeDtypeStruct((1,), f32)),
        in_specs=[pl.BlockSpec(memory_space=pltpu.HBM)] * 2 + [spec] * 8,
        out_specs=(spec, pl.BlockSpec(memory_space=pltpu.SMEM)),
        scratch_shapes=[
            VMEM((C * R, W), f32),
            VMEM((C * R, W), f32),
            VMEM((R * C, W), bf16),
            VMEM(((R + 2 * H) * C, W), bf16),
            VMEM((R * C, W), bf16),
            VMEM(actions.shape, f32),
            VMEM((G, K, CH, W), f32),
            VMEM(((R + 2 * H) * 3 * C, W), bf16),
            VMEM(((R + 2 * H) * 3 * C, W), bf16),
            VMEM((layers, Q * C, wide), bf16),
            VMEM((Q * 2 * C, wide), bf16),
            VMEM((R * C, W), f32),
            VMEM((G, 2, L, W), f32),
            VMEM((G, 2, L, W), f32),
            VMEM((K, CH, W), f32),
            VMEM((K, CH, W), f32),
            VMEM((G, K, CH, W), f32),
            VMEM((G, K, CH, W), f32),
            VMEM((8, W), f32),
            VMEM((S, 8, W), f32),
            DMA((2,)),
            DMA((4,)), DMA((4,)),
            DMA((G,)), DMA((G,)),
            DMA((K,)), DMA((K,)),
            DMA((G, K)), DMA((G, K)),
            DMA((S,)), DMA((S,)),
            DMA((G,)), DMA((1,)),
        ],
        compiler_params=pltpu.CompilerParams(
            collective_id=0, has_side_effects=True, vmem_limit_bytes=63 * 1024 * 1024),
    )(
        traj.reshape(C * R, W), start.reshape(C * R, W), actions,
        hw.reshape(-1, hw.shape[-1]), hb, headw.swapaxes(1, 2).reshape(-1, headw.shape[1]),
        cand_b.reshape(1, C), gate_b.reshape(1, C), skip.reshape(1, C), proj,
    )
    return new.reshape(traj.shape), res


def solution(mesh):
    return jax.shard_map(
        functools.partial(body, mesh.shape["tm"], mesh.shape["space"]),
        mesh=mesh,
        in_specs=(
            P("tm", None, "space", None),
            P(None, "space", None),
            P("tm", None),
            P(), P(), P(), P(), P(), P(), P(),
        ),
        out_specs=(P("tm", None, "space", None), P("tm")),
        check_vma=False,
    )
```

```python
import functools

import jax
import jax.numpy as jnp
from jax import lax
from jax.experimental import pallas as pl
from jax.experimental.pallas import tpu as pltpu
from jax.sharding import PartitionSpec as P

MESH = pl.DeviceIdType.MESH
Q = 2
PARTS = 4
VMEM = pltpu.VMEM


def column(row):
    n = row.shape[1]
    eye = lax.broadcasted_iota(jnp.int32, (n, n), 0) == lax.broadcasted_iota(jnp.int32, (n, n), 1)
    return jnp.sum(jnp.where(eye, jnp.broadcast_to(row, (n, n)), 0.0), axis=1, keepdims=True)


def kernel(
    T, S, G, K, C, R, W, layers,
    traj_h, start_h, actions, hw, hb, headw, cand_b, gate_b, skip_r, proj,
    out, res,
    traj, start, sendb, ext, ha, hbuf, wh, wo, start_r, guess, ab, rab, cin, cout, ys, st, part, rpart,
    s_in, s_prior, r_prior, s_ab, r_ab, s_ch, r_ch, s_st, r_st, s_ps, r_ps,
):
    H = layers + 1
    L = R * C // G
    CH = L // K
    NG = T // G
    RG = R // G
    t = lax.axis_index("tm")
    s = lax.axis_index("space")
    g = t // G
    m = lax.rem(t, G)
    base = g * G
    nxt, prv = lax.rem(t + 1, T), lax.rem(t + T - 1, T)
    peers = []
    for tt in (nxt, prv):
        for ds in sorted({0, 1 % S, (S - 1) % S}):
            peers.append((tt, lax.rem(s + ds, S)))
    for p in range(1, G):
        peers.append((base + lax.rem(m + p, G), s))
    for step in (G, T - G):
        if NG > 1:
            peers.append((lax.rem(t + step, T), s))
    for p in range(1, S):
        peers.append((t, lax.rem(s + p, S)))
    load_t = pltpu.make_async_copy(traj_h, traj, s_in.at[0])
    load_s = pltpu.make_async_copy(start_h, start, s_in.at[1])
    load_t.start()
    load_s.start()
    barrier = pltpu.get_barrier_semaphore()
    for peer in peers:
        pl.semaphore_signal(barrier, inc=1, device_id=peer, device_id_type=MESH)

    last = t == T - 1
    load_t.wait()
    load_s.wait()
    for r in range(R):
        begin = start[pl.ds(r, C, stride=R), :]
        start_r[pl.ds(r * C, C), :] = begin
        sendb[pl.ds(r * C, C), :] = jnp.where(last, begin, traj[pl.ds(r, C, stride=R), :]).astype(jnp.bfloat16)

    pl.semaphore_wait(barrier, len(peers))

    def prior_copy(i, src, dst, to):
        return pltpu.make_async_remote_copy(
            src_ref=src, dst_ref=dst, send_sem=s_prior.at[i], recv_sem=r_prior.at[i],
            device_id=(nxt, to), device_id_type=MESH)

    up, down = s > 0, s < S - 1
    to_down = prior_copy(0, sendb.at[pl.ds((R - H) * C, H * C)], ext.at[pl.ds(0, H * C)], lax.rem(s + 1, S))
    to_up = prior_copy(1, sendb.at[pl.ds(0, H * C)], ext.at[pl.ds((R + H) * C, H * C)], lax.rem(s + S - 1, S))
    PR = R // PARTS
    main = [
        prior_copy(2 + i, sendb.at[pl.ds(i * PR * C, PR * C)], ext.at[pl.ds((H + i * PR) * C, PR * C)], s)
        for i in range(PARTS)
    ]

    @pl.when(down)
    def _():
        to_down.start()

    for copy in main:
        copy.start()

    @pl.when(up)
    def _():
        to_up.start()

    wh[...] = jnp.zeros_like(wh)
    wo[...] = jnp.zeros_like(wo)
    taps = [headw[pl.ds(k * C, C), :].astype(jnp.float32).T.astype(jnp.bfloat16) for k in range(9)]
    for q in range(Q):
        for a in range(3):
            for b in range(3):
                at = ((q + a) * 3 + b) * C
                for l in range(layers):
                    wh[l, pl.ds(q * C, C), pl.ds(at, C)] = hw[pl.ds((l * 9 + 3 * a + b) * C, C), :]
                wo[pl.ds(q * 2 * C, 2 * C), pl.ds(at, C)] = taps[3 * a + b]
    act = column(jnp.sum(column(actions[...]) * proj[...], axis=0, keepdims=True))
    biases = [column(hb[pl.ds(l, 1), :]) for l in range(layers)]
    biases[0] = biases[0] + act[:C]
    cb = column(cand_b[...])
    gb = column(gate_b[...]) + act[C:]
    skip = column(skip_r[...])
    lane = lax.broadcasted_iota(jnp.int32, (C, W), 1)

    def put(buf, row, x):
        buf[pl.ds(row * 3 * C, C), :] = jnp.where(lane == 0, 0.0, pltpu.roll(x, 1, 1)).astype(jnp.bfloat16)
        buf[pl.ds(row * 3 * C + C, C), :] = x.astype(jnp.bfloat16)
        buf[pl.ds(row * 3 * C + 2 * C, C), :] = jnp.where(lane == W - 1, 0.0, pltpu.roll(x, W - 1, 1)).astype(jnp.bfloat16)

    upf, downf = up.astype(jnp.float32), down.astype(jnp.float32)

    def arrive(r):
        if r == 0:
            @pl.when(up)
            def _():
                to_down.wait_recv()

            @pl.when(jnp.logical_not(up))
            def _():
                ext[pl.ds(0, H * C), :] = jnp.zeros((H * C, W), jnp.bfloat16)
        elif r == R + H:
            @pl.when(down)
            def _():
                to_up.wait_recv()

            @pl.when(jnp.logical_not(down))
            def _():
                ext[pl.ds((R + H) * C, H * C), :] = jnp.zeros((H * C, W), jnp.bfloat16)
        elif H <= r < R + H and (r - H) % PR == 0:
            main[(r - H) // PR].wait_recv()
        x = ext[pl.ds(r * C, C), :].astype(jnp.float32)
        put(ha, r, x)
        if H <= r < R + H:
            guess[pl.ds((r - H) * C, C), :] = jnp.where(t == 0, start_r[pl.ds((r - H) * C, C), :], x)

    src, dst = ha, hbuf
    wide = (Q + 2) * 3 * C

    def gather(buf, first, count):
        parts = []
        for i in range(count):
            at = (first + Q * i) * 3 * C
            parts.append(buf[pl.ds(at if isinstance(at, int) else pl.multiple_of(at, 3 * C), wide), :])
        return jnp.concatenate(parts, axis=1)

    here = 0
    for l in range(layers):
        rows = R + 2 * (H - 1 - l)
        edge = H - 1 - l
        pairs = rows // Q
        for lo in range(0, pairs, 2):
            count = min(2, pairs - lo)
            if l == 0:
                while here < Q * (lo + count) + 2:
                    arrive(here)
                    here += 1
            o = jnp.dot(wh[l], gather(src, Q * lo, count), preferred_element_type=jnp.float32)
            for i in range(count):
                for q in range(Q):
                    row = Q * (lo + i) + q
                    pre = o[q * C:(q + 1) * C, i * W:(i + 1) * W] + biases[l]
                    h = pre * jax.nn.sigmoid(pre)
                    if row < edge:
                        h = h * upf
                    elif row >= R + edge:
                        h = h * downf
                    put(dst, row, h)
        src, dst = dst, src

    def ab_copy(p, j):
        return pltpu.make_async_remote_copy(
            src_ref=ab.at[j], dst_ref=rab.at[m], send_sem=s_ab.at[p], recv_sem=r_ab.at[p],
            device_id=(base + j, s), device_id_type=MESH)

    acc = jnp.zeros((C, W), jnp.float32)
    for p in range(1, G + 1):
        j = lax.rem(m + p, G)
        for lo in range(0, RG // Q, 2):
            count = min(2, RG // Q - lo)
            o = jnp.dot(wo[...], gather(src, j * RG + Q * lo, count), preferred_element_type=jnp.float32)
            for i in range(count):
                for q in range(Q):
                    own = Q * (lo + i) + q
                    row = j * RG + own
                    hd = o[q * 2 * C:(q + 1) * 2 * C, i * W:(i + 1) * W]
                    x = guess[pl.ds(pl.multiple_of(row * C, C), C), :]
                    cand = jnp.tanh(hd[:C] + cb + skip * x)
                    gate = jax.nn.sigmoid(hd[C:] + gb)
                    f = gate * x + (1.0 - gate) * cand
                    jac = gate + (1.0 - gate) * (1.0 - cand * cand) * skip
                    d = traj[pl.ds(row, C, stride=R), :] - f
                    acc = acc + d * d
                    ab[j, 0, pl.ds(own * C, C), :] = jac
                    ab[j, 1, pl.ds(own * C, C), :] = f - jac * x
        if p < G:
            ab_copy(p, j).start()
    rab[m] = ab[m]
    part[...] = jnp.sum(acc.reshape(C // 8, 8, W), axis=0)

    def ps_copy(p):
        return pltpu.make_async_remote_copy(
            src_ref=part, dst_ref=rpart.at[p - 1], send_sem=s_ps.at[p - 1], recv_sem=r_ps.at[p - 1],
            device_id=(t, lax.rem(s + p, S)), device_id_type=MESH)

    for p in range(1, S):
        ps_copy(p).start()
    for p in range(1, G):
        ab_copy(p, lax.rem(m + p, G)).wait_recv()

    def chain(k):
        return pltpu.make_async_remote_copy(
            src_ref=cout.at[k], dst_ref=cin.at[k], send_sem=s_ch.at[k], recv_sem=r_ch.at[k],
            device_id=(lax.rem(t + G, T), s), device_id_type=MESH)

    def st_copy(p, k):
        j = lax.rem(m + p, G)
        return pltpu.make_async_remote_copy(
            src_ref=ys.at[j, k], dst_ref=st.at[m, k], send_sem=s_st.at[p, k], recv_sem=r_st.at[p, k],
            device_id=(base + j, s), device_id_type=MESH)

    for k in range(K):
        @pl.when(g == 0)
        def _():
            cin[k] = start_r[pl.ds(m * L + k * CH, CH), :]

        @pl.when(g > 0)
        def _():
            chain(k).wait_recv()

        y = cin[k]
        for j in range(G):
            ys[j, k] = y
            y = rab[j, 0, pl.ds(k * CH, CH), :] * y + rab[j, 1, pl.ds(k * CH, CH), :]
        cout[k] = y

        @pl.when(g < NG - 1)
        def _():
            chain(k).start()

        @pl.when(g == NG - 1)
        def _():
            for p in range(1, G):
                st_copy(p, k).start()

    @pl.when(g < NG - 1)
    def _():
        for k in range(K):
            for p in range(1, G):
                st_copy(p, k).start()

    total = part[...]
    for p in range(1, S):
        ps_copy(p).wait_recv()
        total = total + rpart[p - 1]
    res[0] = jnp.sum(total) * (1.0 / (C * R * S * W))

    for k in range(K):
        for p in range(G):
            j = lax.rem(m + G - p, G)
            if p > 0:
                st_copy(p, k).wait_recv()
                y = st[j, k]
            else:
                y = ys[m, k]
            for i in range(CH // C):
                own = k * (CH // C) + i
                out[pl.ds(j * RG + own, C, stride=R), :] = (
                    ab[j, 0, pl.ds(own * C, C), :] * y[i * C:(i + 1) * C] + ab[j, 1, pl.ds(own * C, C), :])

    for copy in main:
        copy.wait_send()

    @pl.when(down)
    def _():
        to_down.wait_send()

    @pl.when(up)
    def _():
        to_up.wait_send()

    for p in range(1, S):
        ps_copy(p).wait_send()
    for p in range(1, G):
        ab_copy(p, lax.rem(m + p, G)).wait_send()
        for k in range(K):
            st_copy(p, k).wait_send()

    @pl.when(g < NG - 1)
    def _():
        for k in range(K):
            chain(k).wait_send()


def group_of(T, R):
    best = 1
    for n in range(1, T + 1):
        if T % n == 0 and R % n == 0 and n * n <= T:
            best = n
    return best


def body(T, S, traj, start, actions, hw, hb, headw, cand_b, gate_b, skip, proj):
    steps, C, R, W = traj.shape
    layers = hw.shape[0]
    G = group_of(T, R)
    K = R // G
    H = layers + 1
    L = R * C // G
    CH = L // K
    f32, bf16 = jnp.float32, jnp.bfloat16
    wide = (Q + 2) * 3 * C
    DMA = pltpu.SemaphoreType.DMA
    spec = pl.BlockSpec(memory_space=VMEM)
    new, res = pl.pallas_call(
        functools.partial(kernel, T, S, G, K, C, R, W, layers),
        out_shape=(VMEM((C * R, W), f32), jax.ShapeDtypeStruct((1,), f32)),
        in_specs=[pl.BlockSpec(memory_space=pltpu.HBM)] * 2 + [spec] * 8,
        out_specs=(spec, pl.BlockSpec(memory_space=pltpu.SMEM)),
        scratch_shapes=[
            VMEM((C * R, W), f32),
            VMEM((C * R, W), f32),
            VMEM((R * C, W), bf16),
            VMEM(((R + 2 * H) * C, W), bf16),
            VMEM(((R + 2 * H) * 3 * C, W), bf16),
            VMEM(((R + 2 * H) * 3 * C, W), bf16),
            VMEM((layers, Q * C, wide), bf16),
            VMEM((Q * 2 * C, wide), bf16),
            VMEM((R * C, W), f32),
            VMEM((R * C, W), f32),
            VMEM((G, 2, L, W), f32),
            VMEM((G, 2, L, W), f32),
            VMEM((K, CH, W), f32),
            VMEM((K, CH, W), f32),
            VMEM((G, K, CH, W), f32),
            VMEM((G, K, CH, W), f32),
            VMEM((8, W), f32),
            VMEM((max(S - 1, 1), 8, W), f32),
            DMA((2,)),
            DMA((2 + PARTS,)), DMA((2 + PARTS,)),
            DMA((G,)), DMA((G,)),
            DMA((K,)), DMA((K,)),
            DMA((G, K)), DMA((G, K)),
            DMA((max(S - 1, 1),)), DMA((max(S - 1, 1),)),
        ],
        compiler_params=pltpu.CompilerParams(
            collective_id=0, has_side_effects=True, vmem_limit_bytes=63 * 1024 * 1024),
    )(
        traj.reshape(C * R, W), start.reshape(C * R, W), actions,
        hw.reshape(-1, hw.shape[-1]), hb, headw.swapaxes(1, 2).reshape(-1, headw.shape[1]),
        cand_b.reshape(1, C), gate_b.reshape(1, C), skip.reshape(1, C), proj,
    )
    return new.reshape(traj.shape), res


def solution(mesh):
    return jax.shard_map(
        functools.partial(body, mesh.shape["tm"], mesh.shape["space"]),
        mesh=mesh,
        in_specs=(
            P("tm", None, "space", None),
            P(None, "space", None),
            P("tm", None),
            P(), P(), P(), P(), P(), P(), P(),
        ),
        out_specs=(P("tm", None, "space", None), P("tm")),
        check_vma=False,
    )
```
